32 devices in a mesh: psg: 16 (over z, y, core), row: 2 (over x).
Axes of the slice: x: 2, y: 2, z: 4, core: 2. Of those that a mesh axis runs over, the one named last changes fastest.
Arguments:
- psg_len: int32 [32], P('psg'), may hold values from 128 to 512, as said below
- offsets: int32 [32], P('psg'), may hold values from 0 to 1023
- p_query: bfloat16 [32, 512, 8192], P('psg', None, 'row'), may hold values from -8 to 8
- passage_key: bfloat16 [32, 512, 1024], P('psg', None, 'row'), may hold values from -8 to 8
- passage_value: bfloat16 [32, 512, 1024], P('psg', None, 'row'), may hold values from -6 to 6
- p_grad: bfloat16 [32, 512, 8192], P('psg', None, 'row'), may hold values from -6 to 6
- a_query: bfloat16 [64, 8192], P('row'), may hold values from -8 to 8
- a_grad: bfloat16 [64, 8192], P('row'), may hold values from -6 to 6
Outputs:
- p_out: bfloat16 [32, 512, 8192], P('psg', None, 'row')
- p_dq: bfloat16 [32, 512, 8192], P('psg', None, 'row')
- p_dk: bfloat16 [32, 512, 1024], P('psg', None, 'row')
- p_dv: bfloat16 [32, 512, 1024], P('psg', None, 'row')
- a_out: bfloat16 [64, 8192], P('row')
- a_dq: bfloat16 [64, 8192], P('row')
The draws below stay inside these ranges and needn't reach their ends.
Inputs may be any that keep to these rules, and one draw needn't show every extreme that they name: `psg_len`: in every draw some passage holds exactly 512 tokens; a passage's tokens fill its first slots.
All inputs are finite; a program needn't handle non-finite values.
Results may differ from the reference program's by a relative error of at most 0.024.
Values may be sent and summed in bfloat16 or wider, within the bound.
A program may use at most 256 MiB of HBM per device.

```python
import math
import jax
import jax.numpy as jnp
from jax import lax

QUERY_HEAD_COUNT = 64
KEY_VALUE_HEADS = 8
HEAD_SIZE = 128
PASSAGE_SLOTS = 512
PASSAGE_COUNT = 32
ANSWER_TOKENS = 64


def draw_psg_len(key, part):
    key = jax.random.fold_in(key, 5)
    lengths = jax.random.randint(key, (PASSAGE_COUNT,), PASSAGE_SLOTS // 4, PASSAGE_SLOTS + 1)
    longest = jax.random.randint(jax.random.fold_in(key, 1), (), 0, PASSAGE_COUNT)
    return lengths.at[longest].set(PASSAGE_SLOTS).astype(jnp.int32)


def draw_passage_key(key, part):
    key = jax.random.fold_in(key, 3)
    value_entries = jnp.clip(jax.random.normal(key, (PASSAGE_COUNT, PASSAGE_SLOTS, KEY_VALUE_HEADS, HEAD_SIZE), jnp.float32), -8.0, 8.0)
    return value_entries.reshape(PASSAGE_COUNT, PASSAGE_SLOTS, KEY_VALUE_HEADS * HEAD_SIZE).astype(jnp.bfloat16)


def draw_p_query(key, part):
    key = jax.random.fold_in(key, 4)
    query_groups = QUERY_HEAD_COUNT // KEY_VALUE_HEADS
    value_entries = jnp.clip(jax.random.normal(key, (PASSAGE_COUNT, PASSAGE_SLOTS, KEY_VALUE_HEADS, query_groups, HEAD_SIZE), jnp.float32), -8.0, 8.0)
    return value_entries.reshape(PASSAGE_COUNT, PASSAGE_SLOTS, QUERY_HEAD_COUNT * HEAD_SIZE).astype(jnp.bfloat16)


def draw_a_query(key, part):
    key = jax.random.fold_in(key, 6)
    query_groups = QUERY_HEAD_COUNT // KEY_VALUE_HEADS
    value_entries = jnp.clip(jax.random.normal(key, (ANSWER_TOKENS, KEY_VALUE_HEADS, query_groups, HEAD_SIZE), jnp.float32), -8.0, 8.0)
    return value_entries.reshape(ANSWER_TOKENS, QUERY_HEAD_COUNT * HEAD_SIZE).astype(jnp.bfloat16)


def plant(values, own_key, smallest, largest):
    index_at = [jax.random.randint(jax.random.fold_in(own_key, axis), (), 0, length) for axis, length in enumerate(values.shape)]
    widest = values.shape.index(max(values.shape))
    neighbour = index_at[:widest] + [(index_at[widest] + 1) % values.shape[widest]] + index_at[widest + 1:]
    return values.at[tuple(index_at)].set(smallest).at[tuple(neighbour)].set(largest)


def level_of(rng, dims, split, least, top_value):
    factor_of, own = 1.0, jax.random.fold_in(rng, 6)
    for axis_at, shards_of in split:
        draws = jnp.exp(jax.random.uniform(jax.random.fold_in(own, axis_at), (shards_of,), jnp.float32, least / len(split), top_value / len(split)))
        factor_of = factor_of * jnp.repeat(draws, dims[axis_at] // shards_of).reshape([-1 if axis == axis_at else 1 for axis in range(len(dims))])
    return factor_of


def gaussian(key, dims, spread, limit, cuts=(), held_as=jnp.bfloat16):
    drawn = spread * jax.random.normal(key, dims, jnp.float32)
    if cuts:
        drawn = drawn * level_of(key, dims, cuts, -0.22, 0.18)
    return jnp.clip(drawn, -limit, limit).astype(held_as)


def setup_inputs(seed: int = 0) -> dict:
    key_list = jax.random.split(jax.random.key(seed), 9)
    psg_len = draw_psg_len(jax.random.fold_in(key_list[8], 71), 0)
    offsets = plant(jax.random.randint(key_list[1], (PASSAGE_COUNT,), 0, 2 * PASSAGE_SLOTS), jax.random.fold_in(key_list[1], 1), 0, (2 * PASSAGE_SLOTS) - 1).astype(jnp.int32)
    p_query = draw_p_query(jax.random.fold_in(key_list[8], 71), 0)
    passage_key = draw_passage_key(jax.random.fold_in(key_list[8], 71), 0)
    passage_value = gaussian(key_list[4], (PASSAGE_COUNT, PASSAGE_SLOTS, KEY_VALUE_HEADS * HEAD_SIZE), 1.0, 6.0, ((0, 16), (2, 2)))
    p_grad = gaussian(key_list[5], (PASSAGE_COUNT, PASSAGE_SLOTS, QUERY_HEAD_COUNT * HEAD_SIZE), 1.0, 6.0, ((0, 16), (2, 2)))
    a_query = draw_a_query(jax.random.fold_in(key_list[8], 71), 0)
    a_grad = gaussian(key_list[7], (ANSWER_TOKENS, QUERY_HEAD_COUNT * HEAD_SIZE), 1.0, 6.0, ((0, 2),))
    return dict(psg_len=psg_len, offsets=offsets, p_query=p_query, passage_key=passage_key, passage_value=passage_value, p_grad=p_grad, a_query=a_query, a_grad=a_grad)


ROPE_BASE = 500000.0
SCALE_FACTOR = 8.0
LOW_FACTOR = 1.0
HIGH_FACTOR = 4.0
OLD_CONTEXT = 8192.0
FILL_VALUE = -1e+30

def rope_freq(half_dim):
    step_index = jnp.arange(half_dim, dtype=jnp.float32)
    base_freq = jnp.exp(step_index * (-math.log(ROPE_BASE) / half_dim))
    wavelength = 2.0 * math.pi / base_freq
    smooth = (OLD_CONTEXT / wavelength - LOW_FACTOR) / (HIGH_FACTOR - LOW_FACTOR)
    blended = (1.0 - smooth) * base_freq / SCALE_FACTOR + smooth * base_freq
    return jnp.where(wavelength < OLD_CONTEXT / HIGH_FACTOR, base_freq, jnp.where(wavelength > OLD_CONTEXT / LOW_FACTOR, base_freq / SCALE_FACTOR, blended))

def apply_rotation(vectors, position_shift, direction):
    half_dim = vectors.shape[-1] // 2
    angles = position_shift * rope_freq(half_dim)
    cosine = jnp.cos(angles)
    sine_part = direction * jnp.sin(angles)
    front_half = vectors[..., :half_dim]
    back_half = vectors[..., half_dim:]
    return jnp.concatenate([front_half * cosine - back_half * sine_part, back_half * cosine + front_half * sine_part], axis=-1)

def widen_heads(weights):
    return jnp.repeat(weights, HEAD_SIZE, axis=-1)

def heads_first(stats, kv_heads, query_groups):
    row_count = stats.shape[0]
    return jnp.transpose(stats.reshape(row_count, kv_heads, query_groups), (1, 2, 0))

def passage_core(query_rows, key_rows, value_rows, grad_rows, length):
    single_float = jnp.float32
    row_count = query_rows.shape[0]
    kv_heads = key_rows.shape[1] // HEAD_SIZE
    query_groups = query_rows.shape[1] // key_rows.shape[1]
    score_scale = 1.0 / math.sqrt(HEAD_SIZE)
    queries = query_rows.reshape(row_count, kv_heads, query_groups, HEAD_SIZE).astype(single_float)
    key_vecs = key_rows.reshape(row_count, kv_heads, HEAD_SIZE).astype(single_float)
    value_vecs = value_rows.reshape(row_count, kv_heads, HEAD_SIZE).astype(single_float)
    grads_in = grad_rows.reshape(row_count, kv_heads, query_groups, HEAD_SIZE)
    positions = jnp.arange(row_count)
    row_ok = positions < length
    allowed = (positions[None, :] <= positions[:, None]) & row_ok[None, :]
    scores = jnp.einsum('ikgd,jkd->kgij', queries, key_vecs) * score_scale
    scores = jnp.where(allowed, scores, FILL_VALUE)
    row_max = lax.optimization_barrier(jnp.max(scores, axis=-1, keepdims=True))
    weights = jnp.where(allowed, jnp.exp(scores - row_max), 0.0)
    totals = lax.optimization_barrier(jnp.sum(weights, axis=-1, keepdims=True))
    prob_rows = weights / totals
    prob_low = prob_rows.astype(jnp.bfloat16)
    output = jnp.einsum('kgij,jkd->ikgd', prob_low.astype(single_float), value_vecs)
    output_low = jnp.where(row_ok[:, None, None, None], output, 0.0).astype(jnp.bfloat16)
    grads_masked = jnp.where(row_ok[:, None, None, None], grads_in, jnp.zeros_like(grads_in))
    grads_wide = grads_masked.astype(single_float)
    delta_rows = lax.optimization_barrier(jnp.sum(grads_wide * output_low.astype(single_float), axis=-1))
    delta_rows = jnp.transpose(delta_rows, (1, 2, 0))[..., None]
    dprob_rows = jnp.einsum('ikgd,jkd->kgij', grads_wide, value_vecs)
    dscore_low = (prob_rows * (dprob_rows - delta_rows)).astype(jnp.bfloat16).astype(single_float)
    query_grad = jnp.einsum('kgij,jkd->ikgd', dscore_low, key_vecs) * score_scale
    key_grad = jnp.einsum('kgij,ikgd->jkd', dscore_low, queries) * score_scale
    value_grad = jnp.einsum('kgij,ikgd->jkd', prob_low.astype(single_float), grads_wide)
    return (output_low.reshape(row_count, -1), query_grad.astype(jnp.bfloat16).reshape(row_count, -1), key_grad.reshape(row_count, -1), value_grad.reshape(row_count, -1))

def answer_part(query_rows, key_rotation, value_rows, length):
    single_float = jnp.float32
    row_count = query_rows.shape[0]
    key_count = key_rotation.shape[0]
    kv_heads = key_rotation.shape[1] // HEAD_SIZE
    query_groups = query_rows.shape[1] // key_rotation.shape[1]
    score_scale = 1.0 / math.sqrt(HEAD_SIZE)
    queries = query_rows.reshape(row_count, kv_heads, query_groups, HEAD_SIZE).astype(single_float)
    key_vecs = key_rotation.reshape(key_count, kv_heads, HEAD_SIZE).astype(single_float)
    value_vecs = value_rows.reshape(key_count, kv_heads, HEAD_SIZE).astype(single_float)
    key_ok = jnp.arange(key_count) < length
    scores = jnp.einsum('rkgd,jkd->kgrj', queries, key_vecs) * score_scale
    scores = jnp.where(key_ok, scores, FILL_VALUE)
    part_max = lax.optimization_barrier(jnp.max(scores, axis=-1))
    weights = jnp.where(key_ok, jnp.exp(scores - part_max[..., None]), 0.0)
    part_total = lax.optimization_barrier(jnp.sum(weights, axis=-1))
    part_out = jnp.einsum('kgrj,jkd->rkgd', weights.astype(jnp.bfloat16).astype(single_float), value_vecs)
    return (part_out.reshape(row_count, -1), jnp.transpose(part_max, (2, 0, 1)).reshape(row_count, -1), jnp.transpose(part_total, (2, 0, 1)).reshape(row_count, -1))

def answer_backward(query_rows, grad_rows, lse_rows, delta_rows, key_rotation, value_rows, length):
    single_float = jnp.float32
    row_count = query_rows.shape[0]
    key_count = key_rotation.shape[0]
    kv_heads = key_rotation.shape[1] // HEAD_SIZE
    query_groups = query_rows.shape[1] // key_rotation.shape[1]
    score_scale = 1.0 / math.sqrt(HEAD_SIZE)
    queries = query_rows.reshape(row_count, kv_heads, query_groups, HEAD_SIZE).astype(single_float)
    grads_in = grad_rows.reshape(row_count, kv_heads, query_groups, HEAD_SIZE).astype(single_float)
    key_vecs = key_rotation.reshape(key_count, kv_heads, HEAD_SIZE).astype(single_float)
    value_vecs = value_rows.reshape(key_count, kv_heads, HEAD_SIZE).astype(single_float)
    key_ok = jnp.arange(key_count) < length
    scores = jnp.einsum('rkgd,jkd->kgrj', queries, key_vecs) * score_scale
    lse_heads = heads_first(lse_rows, kv_heads, query_groups)[..., None]
    prob_rows = jnp.where(key_ok, jnp.exp(scores - lse_heads), 0.0)
    dprob_rows = jnp.einsum('rkgd,jkd->kgrj', grads_in, value_vecs)
    delta_heads = heads_first(delta_rows, kv_heads, query_groups)[..., None]
    dscore_low = (prob_rows * (dprob_rows - delta_heads)).astype(jnp.bfloat16).astype(single_float)
    query_grad = jnp.einsum('kgrj,jkd->rkgd', dscore_low, key_vecs) * score_scale
    key_grad = jnp.einsum('kgrj,rkgd->jkd', dscore_low, queries) * score_scale
    value_grad = jnp.einsum('kgrj,rkgd->jkd', prob_rows.astype(jnp.bfloat16).astype(single_float), grads_in)
    return (query_grad.reshape(row_count, -1), key_grad.reshape(key_count, -1), value_grad.reshape(key_count, -1))

def fold_part(running, new_part):
    acc_out, acc_max, acc_total = running
    new_out, new_max, new_total = new_part
    peak_max = jnp.maximum(acc_max, new_max)
    old_weight = jnp.exp(acc_max - peak_max)
    new_weight = jnp.exp(new_max - peak_max)
    return (acc_out * widen_heads(old_weight) + new_out * widen_heads(new_weight), peak_max, acc_total * old_weight + new_total * new_weight)

def run_passage(per_passage):
    return passage_core(*per_passage)

def reference(psg_len, offsets, p_query, passage_key, passage_value, p_grad, a_query, a_grad):
    single_float = jnp.float32
    p_out, p_dq, pass_dk, pass_dv = lax.map(run_passage, (p_query, passage_key, passage_value, p_grad, psg_len))
    position_shift = offsets.astype(single_float)[:, None, None, None]
    key_rotation = apply_rotation(passage_key.reshape(PASSAGE_COUNT, PASSAGE_SLOTS, KEY_VALUE_HEADS, HEAD_SIZE).astype(single_float), position_shift, 1.0)
    key_rotation = key_rotation.astype(jnp.bfloat16).reshape(PASSAGE_COUNT, PASSAGE_SLOTS, KEY_VALUE_HEADS * HEAD_SIZE)
    feat_width = QUERY_HEAD_COUNT * HEAD_SIZE
    initial = (jnp.zeros((ANSWER_TOKENS, feat_width), single_float), jnp.full((ANSWER_TOKENS, QUERY_HEAD_COUNT), FILL_VALUE, single_float), jnp.zeros((ANSWER_TOKENS, QUERY_HEAD_COUNT), single_float))

    def forward_step(running, per_passage):
        return (fold_part(running, answer_part(a_query, *per_passage)), None)
    combined, unused_out = lax.scan(forward_step, initial, (key_rotation, passage_value, psg_len))
    acc_out, acc_max, acc_total = combined
    a_out = (acc_out / widen_heads(acc_total)).astype(jnp.bfloat16)
    lse_rows = acc_max + jnp.log(acc_total)
    delta_rows = lax.optimization_barrier(jnp.sum((a_grad.astype(single_float) * a_out.astype(single_float)).reshape(ANSWER_TOKENS, QUERY_HEAD_COUNT, HEAD_SIZE), axis=-1))

    def backward_step(dq_acc, per_passage):
        query_grad, key_grad, value_grad = answer_backward(a_query, a_grad, lse_rows, delta_rows, *per_passage)
        return (dq_acc + query_grad, (key_grad, value_grad))
    dq_sum, key_terms = lax.scan(backward_step, jnp.zeros((ANSWER_TOKENS, feat_width), single_float), (key_rotation, passage_value, psg_len))
    answer_key_gradient, ans_dv = key_terms
    reverse_rotation = apply_rotation(answer_key_gradient.reshape(PASSAGE_COUNT, PASSAGE_SLOTS, KEY_VALUE_HEADS, HEAD_SIZE), position_shift, -1.0).reshape(PASSAGE_COUNT, PASSAGE_SLOTS, KEY_VALUE_HEADS * HEAD_SIZE)
    p_dk = (pass_dk + reverse_rotation).astype(jnp.bfloat16)
    p_dv = (pass_dv + ans_dv).astype(jnp.bfloat16)
    a_dq = dq_sum.astype(jnp.bfloat16)
    return (p_out, p_dq, p_dk, p_dv, a_out, a_dq)
```

```python
import functools
import math

import jax
import jax.numpy as jnp
from jax import lax
from jax.experimental import pallas as pl
from jax.experimental.pallas import tpu as pltpu
from jax.sharding import PartitionSpec as P

HEAD_SIZE = 128
ROPE_BASE = 500000.0
SCALE_FACTOR = 8.0
LOW_FACTOR = 1.0
HIGH_FACTOR = 4.0
OLD_CONTEXT = 8192.0
FILL_VALUE = -1e30
LOG2E = math.log2(math.e)
SCALE = 1.0 / math.sqrt(HEAD_SIZE)
BLOCK = 128
F32 = jnp.float32
BF16 = jnp.bfloat16
VMEM_LIMIT = 50 * 1024 * 1024


def rope_freq(half_dim):
    step_index = jnp.arange(half_dim, dtype=F32)
    base_freq = jnp.exp(step_index * (-math.log(ROPE_BASE) / half_dim))
    wavelength = 2.0 * math.pi / base_freq
    smooth = (OLD_CONTEXT / wavelength - LOW_FACTOR) / (HIGH_FACTOR - LOW_FACTOR)
    blended = (1.0 - smooth) * base_freq / SCALE_FACTOR + smooth * base_freq
    return jnp.where(
        wavelength < OLD_CONTEXT / HIGH_FACTOR,
        base_freq,
        jnp.where(wavelength > OLD_CONTEXT / LOW_FACTOR, base_freq / SCALE_FACTOR, blended),
    )


def mm_nt(a, b):
    return lax.dot_general(a, b, (((1,), (1,)), ((), ())), preferred_element_type=F32)


def mm(a, b):
    return lax.dot_general(a, b, (((1,), (0,)), ((), ())), preferred_element_type=F32)


def head_stack(ref_rows, heads):
    return jnp.concatenate([ref_rows(h) for h in heads], axis=0)


def passage_kernel(first, adds, len_ref, q_ref, k_ref, v_ref, g_ref, *rest):
    if adds:
        ak_ref, av_ref = rest[:2]
    o_ref, dq_ref, dk_ref, dv_ref, dk_acc, dv_acc = rest[-6:]
    slots = k_ref.shape[1]
    groups = q_ref.shape[2] // HEAD_SIZE
    length = len_ref[first + pl.program_id(0)]
    key = k_ref[0]
    val = v_ref[0]
    key_t = key.T
    val_t = val.T
    if adds:
        dk_acc[...] = ak_ref[0]
        dv_acc[...] = av_ref[0]
    else:
        dk_acc[...] = jnp.zeros_like(dk_acc)
        dv_acc[...] = jnp.zeros_like(dv_acc)
    width = 2 * BLOCK
    causal = lax.broadcasted_iota(jnp.int32, (BLOCK, width), 0) <= (
        lax.broadcasted_iota(jnp.int32, (BLOCK, width), 1) & (BLOCK - 1)
    )
    lane_pos = lax.broadcasted_iota(jnp.int32, (1, width), 1) & (BLOCK - 1)
    row_pos = lax.broadcasted_iota(jnp.int32, (width, HEAD_SIZE), 0) & (BLOCK - 1)
    for b in range(slots // BLOCK):
        lo = b * BLOCK
        hi = lo + BLOCK

        @pl.when(length <= lo)
        def _():
            o_ref[0, lo:hi, :] = jnp.zeros((BLOCK, o_ref.shape[2]), BF16)
            dq_ref[0, lo:hi, :] = jnp.zeros((BLOCK, o_ref.shape[2]), BF16)

        @pl.when(length > lo)
        def _():
            row_ok = row_pos + lo < length
            lane_ok = lane_pos + lo < length
            qs, gs, ps, dss = [], [], [], []
            for h in range(0, groups, 2):
                heads = (h, h + 1)
                q2 = head_stack(lambda x: q_ref[0, lo:hi, x * HEAD_SIZE : (x + 1) * HEAD_SIZE], heads)
                g2 = head_stack(lambda x: g_ref[0, lo:hi, x * HEAD_SIZE : (x + 1) * HEAD_SIZE], heads)
                g2 = jnp.where(row_ok, g2.astype(F32), 0.0).astype(BF16)
                s = mm_nt(key[:hi], q2)
                tail = jnp.where(causal, s[lo:], FILL_VALUE)
                s = tail if b == 0 else jnp.concatenate([s[:lo], tail], axis=0)
                s = s * (SCALE * LOG2E)
                m = jnp.max(s, axis=0, keepdims=True)
                e = jnp.exp2(s - m)
                p = e * (1.0 / jnp.sum(e, axis=0, keepdims=True))
                pb = p.astype(BF16)
                dp = mm_nt(val[:hi], g2)
                delta = jnp.sum(p * dp, axis=0, keepdims=True)
                ds = (p * (dp - delta)).astype(BF16)
                o = jnp.where(lane_ok, mm(val_t[:, :hi], pb), 0.0).T.astype(BF16)
                dq = (mm(key_t[:, :hi], ds) * SCALE).T.astype(BF16)
                for n, x in enumerate(heads):
                    cols = slice(x * HEAD_SIZE, (x + 1) * HEAD_SIZE)
                    o_ref[0, lo:hi, cols] = o[n * BLOCK : (n + 1) * BLOCK]
                    dq_ref[0, lo:hi, cols] = dq[n * BLOCK : (n + 1) * BLOCK]
                qs.append(q2)
                gs.append(g2)
                ps.append(pb)
                dss.append(ds)
            dk_acc[:hi] += mm(jnp.concatenate(dss, axis=1), jnp.concatenate(qs, axis=0)) * SCALE
            dv_acc[:hi] += mm(jnp.concatenate(ps, axis=1), jnp.concatenate(gs, axis=0))

    dk_ref[0] = dk_acc[...].astype(dk_ref.dtype)
    dv_ref[0] = dv_acc[...].astype(dv_ref.dtype)


def run_passages(lengths, query, key, val, grad):
    count, slots, feat = query.shape
    kv = key.shape[2] // HEAD_SIZE
    group_width = feat // kv
    wide = pl.BlockSpec((1, slots, group_width), lambda p, g: (p, 0, g))
    thin = pl.BlockSpec((1, slots, HEAD_SIZE), lambda p, g: (p, 0, g))
    return pl.pallas_call(
        functools.partial(passage_kernel, 0, False),
        grid=(count, kv),
        in_specs=[pl.BlockSpec(memory_space=pltpu.SMEM), wide, thin, thin, wide],
        out_specs=[wide, wide, thin, thin],
        out_shape=[
            jax.ShapeDtypeStruct(query.shape, BF16),
            jax.ShapeDtypeStruct(query.shape, BF16),
            jax.ShapeDtypeStruct(key.shape, F32),
            jax.ShapeDtypeStruct(key.shape, F32),
        ],
        scratch_shapes=[pltpu.VMEM((slots, HEAD_SIZE), F32)] * 2,
        compiler_params=pltpu.CompilerParams(vmem_limit_bytes=VMEM_LIMIT),
        cost_estimate=pl.CostEstimate(
            flops=8 * count * slots * slots * feat,
            bytes_accessed=8 * count * slots * feat,
            transcendentals=count * slots * slots * feat // HEAD_SIZE,
        ),
        name="passages",
    )(lengths, query, key, val, grad)


def rotated(key, cos, sin):
    wide = key.astype(F32)
    return (wide * cos + pltpu.roll(wide, HEAD_SIZE // 2, 1) * sin).astype(BF16)


def chunk_heads(tokens):
    return max(1, 256 // tokens)


def stats_kernel(len_ref, cos_ref, sin_ref, q_ref, g_ref, k_ref, v_ref, out_ref):
    count, slots = k_ref.shape[:2]
    tokens = q_ref.shape[0]
    groups = q_ref.shape[1] // HEAD_SIZE
    step = chunk_heads(tokens)
    keys = [rotated(k_ref[p], cos_ref[p], sin_ref[p]) for p in range(count)]
    at = lax.broadcasted_iota(jnp.int32, (slots, step * tokens), 0)
    for h in range(0, groups, step):
        heads = range(h, h + step)
        q2 = head_stack(lambda x: q_ref[:, x * HEAD_SIZE : (x + 1) * HEAD_SIZE], heads)
        g2 = head_stack(lambda x: g_ref[:, x * HEAD_SIZE : (x + 1) * HEAD_SIZE], heads)
        lses, deltas = [], []
        for p in range(count):
            s = mm_nt(keys[p], q2)
            s = jnp.where(at < len_ref[p], s, FILL_VALUE) * (SCALE * LOG2E)
            m = jnp.max(s, axis=0, keepdims=True)
            e = jnp.exp2(s - m)
            total = jnp.sum(e, axis=0, keepdims=True)
            dp = mm_nt(v_ref[p], g2)
            lses.append(m + jnp.log2(total))
            deltas.append(jnp.sum(e * dp, axis=0, keepdims=True) / total)
        lse, delta = merge(jnp.concatenate(lses, axis=0), jnp.concatenate(deltas, axis=0))
        cols = slice(h * tokens, (h + step) * tokens)
        out_ref[0, 0:1, cols] = lse
        out_ref[0, 1:2, cols] = delta


def merge(lses, deltas):
    m = jnp.max(lses, axis=0, keepdims=True)
    w = jnp.exp2(lses - m)
    total = jnp.sum(w, axis=0, keepdims=True)
    return m + jnp.log2(total), jnp.sum(w * deltas, axis=0, keepdims=True) / total


def run_stats(lengths, cos, sin, query, grad, key, val):
    count, slots, feat = key.shape
    kv = feat // HEAD_SIZE
    tokens, width = query.shape
    groups = width // feat
    wide = pl.BlockSpec((tokens, width // kv), lambda g: (0, g))
    thin = pl.BlockSpec((count, slots, HEAD_SIZE), lambda g: (0, 0, g))
    whole = pl.BlockSpec((count, 1, HEAD_SIZE), lambda g: (0, 0, 0))
    return pl.pallas_call(
        stats_kernel,
        grid=(kv,),
        in_specs=[pl.BlockSpec(memory_space=pltpu.SMEM), whole, whole, wide, wide, thin, thin],
        out_specs=pl.BlockSpec((1, 2, groups * tokens), lambda g: (g, 0, 0)),
        out_shape=jax.ShapeDtypeStruct((kv, 2, groups * tokens), F32),
        compiler_params=pltpu.CompilerParams(vmem_limit_bytes=VMEM_LIMIT),
        cost_estimate=pl.CostEstimate(
            flops=4 * count * slots * tokens * width,
            bytes_accessed=4 * count * slots * feat + 4 * tokens * width,
            transcendentals=count * slots * tokens * groups * kv,
        ),
        name="answer_stats",
    )(lengths, cos, sin, query, grad, key, val)


def grads_kernel(
    len_ref, cos_ref, sin_ref, q_ref, g_ref, k_ref, v_ref, stat_ref, pk_ref, pv_ref,
    o_ref, dq_ref, dk_ref, dv_ref, dk_acc, dv_acc,
):
    count, slots = k_ref.shape[:2]
    tokens = q_ref.shape[0]
    groups = q_ref.shape[1] // HEAD_SIZE
    step = chunk_heads(tokens)
    keys = [rotated(k_ref[p], cos_ref[p], sin_ref[p]) for p in range(count)]
    keys_t = [k.T for k in keys]
    vals_t = [v_ref[p].T for p in range(count)]
    at = lax.broadcasted_iota(jnp.int32, (slots, step * tokens), 0)
    for h in range(0, groups, step):
        heads = range(h, h + step)
        cols = slice(h * tokens, (h + step) * tokens)
        q2 = head_stack(lambda x: q_ref[:, x * HEAD_SIZE : (x + 1) * HEAD_SIZE], heads)
        g2 = head_stack(lambda x: g_ref[:, x * HEAD_SIZE : (x + 1) * HEAD_SIZE], heads)
        lse, delta = merge(stat_ref[:, 0, 0, cols], stat_ref[:, 0, 1, cols])
        o_t = dq_t = None
        for p in range(count):
            s = mm_nt(keys[p], q2) * (SCALE * LOG2E)
            prob = jnp.where(at < len_ref[p], jnp.exp2(s - lse), 0.0)
            pb = prob.astype(BF16)
            dp = mm_nt(v_ref[p], g2)
            ds = (prob * (dp - delta)).astype(BF16)
            o_new = mm(vals_t[p], pb)
            dq_new = mm(keys_t[p], ds)
            o_t = o_new if p == 0 else o_t + o_new
            dq_t = dq_new if p == 0 else dq_t + dq_new
            dk_new = mm(ds, q2)
            dv_new = mm(pb, g2)
            if h == 0:
                dk_acc[p] = dk_new
                dv_acc[p] = dv_new
            else:
                dk_acc[p] += dk_new
                dv_acc[p] += dv_new
        o = o_t.T.astype(BF16)
        dq = (dq_t * SCALE).T.astype(BF16)
        for n, x in enumerate(heads):
            out_cols = slice(x * HEAD_SIZE, (x + 1) * HEAD_SIZE)
            o_ref[:, out_cols] = o[n * tokens : (n + 1) * tokens]
            dq_ref[:, out_cols] = dq[n * tokens : (n + 1) * tokens]
    for p in range(count):
        dk = dk_acc[p] * SCALE
        dk = dk * cos_ref[p] - pltpu.roll(dk, HEAD_SIZE // 2, 1) * sin_ref[p]
        dk_ref[p] = (dk + pk_ref[p]).astype(dk_ref.dtype)
        dv_ref[p] = (dv_acc[p] + pv_ref[p]).astype(dv_ref.dtype)


def run_grads(lengths, cos, sin, query, grad, key, val, stats, pass_dk, pass_dv):
    count, slots, feat = key.shape
    kv = feat // HEAD_SIZE
    tokens, width = query.shape
    groups = width // feat
    wide = pl.BlockSpec((tokens, width // kv), lambda g: (0, g))
    thin = pl.BlockSpec((count, slots, HEAD_SIZE), lambda g: (0, 0, g))
    whole = pl.BlockSpec((count, 1, HEAD_SIZE), lambda g: (0, 0, 0))
    stat = pl.BlockSpec((stats.shape[0], 1, 2, groups * tokens), lambda g: (0, g, 0, 0))
    return pl.pallas_call(
        grads_kernel,
        grid=(kv,),
        in_specs=[
            pl.BlockSpec(memory_space=pltpu.SMEM),
            whole, whole, wide, wide, thin, thin, stat, thin, thin,
        ],
        out_specs=[wide, wide, thin, thin],
        out_shape=[
            jax.ShapeDtypeStruct(query.shape, BF16),
            jax.ShapeDtypeStruct(query.shape, BF16),
            jax.ShapeDtypeStruct(key.shape, BF16),
            jax.ShapeDtypeStruct(key.shape, BF16),
        ],
        scratch_shapes=[pltpu.VMEM((count, slots, HEAD_SIZE), F32)] * 2,
        compiler_params=pltpu.CompilerParams(vmem_limit_bytes=VMEM_LIMIT),
        cost_estimate=pl.CostEstimate(
            flops=12 * count * slots * tokens * width,
            bytes_accessed=16 * count * slots * feat + 8 * tokens * width,
            transcendentals=count * slots * tokens * groups * kv,
        ),
        name="answer_grads",
    )(lengths, cos, sin, query, grad, key, val, stats, pass_dk, pass_dv)


def shards(n_psg, n_row, psg_len, offsets, p_query, passage_key, passage_value, p_grad, a_query, a_grad):
    def to_groups(rows):
        got = lax.all_to_all(rows, "row", split_axis=1, concat_axis=0, tiled=True)
        got = got.reshape(n_row, n_psg, -1, got.shape[1])
        return jnp.transpose(got, (1, 0, 2, 3)).reshape(-1, got.shape[3])

    queries = to_groups(a_query)
    grads_in = to_groups(a_grad)
    tokens, width = queries.shape
    share = tokens // (n_psg * n_row)

    angles = offsets.astype(F32)[:, None, None] * rope_freq(HEAD_SIZE // 2)
    cos = jnp.cos(angles)
    sin = jnp.sin(angles)
    cos = jnp.concatenate([cos, cos], axis=-1)
    sin = jnp.concatenate([-sin, sin], axis=-1)

    stats = run_stats(psg_len, cos, sin, queries, grads_in, passage_key, passage_value)
    stats = lax.all_gather(stats, "psg", axis=0)
    p_out, p_dq, pass_dk, pass_dv = run_passages(
        psg_len, p_query, passage_key, passage_value, p_grad
    )
    o_part, dq_part, p_dk, p_dv = run_grads(
        psg_len, cos, sin, queries, grads_in, passage_key, passage_value, stats, pass_dk, pass_dv
    )

    def to_owners(part):
        got = lax.all_to_all(part, ("psg", "row"), split_axis=0, concat_axis=0, tiled=True)
        got = got.reshape(n_psg, n_row, share, width).astype(F32)
        return jnp.sum(got, axis=0).astype(BF16)

    both = jnp.stack([to_owners(o_part), to_owners(dq_part)])
    both = jnp.transpose(both, (0, 2, 1, 3)).reshape(2, share, n_row * width)
    both = lax.all_gather(both, "psg", axis=1, tiled=True)
    return (p_out, p_dq, p_dk, p_dv, both[0], both[1])


def solution(mesh):
    return jax.shard_map(
        functools.partial(shards, mesh.shape["psg"], mesh.shape["row"]),
        mesh=mesh,
        in_specs=(
            P("psg"),
            P("psg"),
            P("psg", None, "row"),
            P("psg", None, "row"),
            P("psg", None, "row"),
            P("psg", None, "row"),
            P("row", None),
            P("row", None),
        ),
        out_specs=(
            P("psg", None, "row"),
            P("psg", None, "row"),
            P("psg", None, "row"),
            P("psg", None, "row"),
            P("row", None),
            P("row", None),
        ),
        check_vma=False,
    )
```

```python
import functools
import math

import jax
import jax.numpy as jnp
from jax import lax
from jax.experimental import pallas as pl
from jax.experimental.pallas import tpu as pltpu
from jax.sharding import PartitionSpec as P

HEAD_SIZE = 128
ROPE_BASE = 500000.0
SCALE_FACTOR = 8.0
LOW_FACTOR = 1.0
HIGH_FACTOR = 4.0
OLD_CONTEXT = 8192.0
FILL_VALUE = -1e30
LOG2E = math.log2(math.e)
SCALE = 1.0 / math.sqrt(HEAD_SIZE)
BLOCK = 128
F32 = jnp.float32
BF16 = jnp.bfloat16
VMEM_LIMIT = 50 * 1024 * 1024


def rope_freq(half_dim):
    step_index = jnp.arange(half_dim, dtype=F32)
    base_freq = jnp.exp(step_index * (-math.log(ROPE_BASE) / half_dim))
    wavelength = 2.0 * math.pi / base_freq
    smooth = (OLD_CONTEXT / wavelength - LOW_FACTOR) / (HIGH_FACTOR - LOW_FACTOR)
    blended = (1.0 - smooth) * base_freq / SCALE_FACTOR + smooth * base_freq
    return jnp.where(
        wavelength < OLD_CONTEXT / HIGH_FACTOR,
        base_freq,
        jnp.where(wavelength > OLD_CONTEXT / LOW_FACTOR, base_freq / SCALE_FACTOR, blended),
    )


def mm_nt(a, b):
    return lax.dot_general(a, b, (((1,), (1,)), ((), ())), preferred_element_type=F32)


def mm(a, b):
    return lax.dot_general(a, b, (((1,), (0,)), ((), ())), preferred_element_type=F32)


def head_stack(ref_rows, heads):
    return jnp.concatenate([ref_rows(h) for h in heads], axis=0)


def passage_kernel(index, len_ref, q_ref, k_ref, v_ref, g_ref, ak_ref, av_ref, *rest):
    o_ref, dq_ref, dk_ref, dv_ref, dk_acc, dv_acc = rest[-6:]
    slots = k_ref.shape[1]
    groups = q_ref.shape[2] // HEAD_SIZE
    length = len_ref[index]
    key = k_ref[0]
    val = v_ref[0]
    key_t = key.T
    val_t = val.T
    dk_acc[...] = ak_ref[0]
    dv_acc[...] = av_ref[0]
    width = 2 * BLOCK
    causal = lax.broadcasted_iota(jnp.int32, (BLOCK, width), 0) <= (
        lax.broadcasted_iota(jnp.int32, (BLOCK, width), 1) & (BLOCK - 1)
    )
    lane_pos = lax.broadcasted_iota(jnp.int32, (1, width), 1) & (BLOCK - 1)
    row_pos = lax.broadcasted_iota(jnp.int32, (width, HEAD_SIZE), 0) & (BLOCK - 1)
    for b in range(slots // BLOCK):
        lo = b * BLOCK
        hi = lo + BLOCK

        @pl.when(length <= lo)
        def _():
            o_ref[0, lo:hi, :] = jnp.zeros((BLOCK, o_ref.shape[2]), BF16)
            dq_ref[0, lo:hi, :] = jnp.zeros((BLOCK, o_ref.shape[2]), BF16)

        @pl.when(length > lo)
        def _():
            row_ok = row_pos + lo < length
            lane_ok = lane_pos + lo < length
            qs, gs, ps, dss = [], [], [], []
            for h in range(0, groups, 2):
                heads = (h, h + 1)
                q2 = head_stack(lambda x: q_ref[0, lo:hi, x * HEAD_SIZE : (x + 1) * HEAD_SIZE], heads)
                g2 = head_stack(lambda x: g_ref[0, lo:hi, x * HEAD_SIZE : (x + 1) * HEAD_SIZE], heads)
                g2 = jnp.where(row_ok, g2.astype(F32), 0.0).astype(BF16)
                s = mm_nt(key[:hi], q2)
                tail = jnp.where(causal, s[lo:], FILL_VALUE)
                s = tail if b == 0 else jnp.concatenate([s[:lo], tail], axis=0)
                s = s * (SCALE * LOG2E)
                m = jnp.max(s, axis=0, keepdims=True)
                e = jnp.exp2(s - m)
                p = e * (1.0 / jnp.sum(e, axis=0, keepdims=True))
                pb = p.astype(BF16)
                dp = mm_nt(val[:hi], g2)
                delta = jnp.sum(p * dp, axis=0, keepdims=True)
                ds = (p * (dp - delta)).astype(BF16)
                o = jnp.where(lane_ok, mm(val_t[:, :hi], pb), 0.0).T.astype(BF16)
                dq = (mm(key_t[:, :hi], ds) * SCALE).T.astype(BF16)
                for n, x in enumerate(heads):
                    cols = slice(x * HEAD_SIZE, (x + 1) * HEAD_SIZE)
                    o_ref[0, lo:hi, cols] = o[n * BLOCK : (n + 1) * BLOCK]
                    dq_ref[0, lo:hi, cols] = dq[n * BLOCK : (n + 1) * BLOCK]
                qs.append(q2)
                gs.append(g2)
                ps.append(pb)
                dss.append(ds)
            dk_acc[:hi] += mm(jnp.concatenate(dss, axis=1), jnp.concatenate(qs, axis=0)) * SCALE
            dv_acc[:hi] += mm(jnp.concatenate(ps, axis=1), jnp.concatenate(gs, axis=0))

    dk_ref[0] = dk_acc[...].astype(dk_ref.dtype)
    dv_ref[0] = dv_acc[...].astype(dv_ref.dtype)


def run_passage(index, lengths, query, key, val, grad, ans_dk, ans_dv, before):
    count, slots, feat = query.shape
    kv = key.shape[2] // HEAD_SIZE
    group_width = feat // kv
    wide = pl.BlockSpec((1, slots, group_width), lambda p, g: (index, 0, g))
    thin = pl.BlockSpec((1, slots, HEAD_SIZE), lambda p, g: (index, 0, g))
    kept = pl.BlockSpec(memory_space=pl.ANY)
    return pl.pallas_call(
        functools.partial(passage_kernel, index),
        grid=(1, kv),
        in_specs=[pl.BlockSpec(memory_space=pltpu.SMEM), wide, thin, thin, wide, thin, thin]
        + [kept] * len(before),
        out_specs=[wide, wide, thin, thin],
        out_shape=[
            jax.ShapeDtypeStruct(query.shape, BF16),
            jax.ShapeDtypeStruct(query.shape, BF16),
            jax.ShapeDtypeStruct(key.shape, BF16),
            jax.ShapeDtypeStruct(key.shape, BF16),
        ],
        input_output_aliases={7 + n: n for n in range(len(before))},
        scratch_shapes=[pltpu.VMEM((slots, HEAD_SIZE), F32)] * 2,
        compiler_params=pltpu.CompilerParams(vmem_limit_bytes=VMEM_LIMIT),
        cost_estimate=pl.CostEstimate(
            flops=16 * slots * slots * feat,
            bytes_accessed=8 * slots * feat,
            transcendentals=slots * slots * feat // HEAD_SIZE,
        ),
        name="passage",
    )(lengths, query, key, val, grad, ans_dk, ans_dv, *before)


def rotated(key, cos, sin):
    wide = key.astype(F32)
    return (wide * cos + pltpu.roll(wide, HEAD_SIZE // 2, 1) * sin).astype(BF16)


def chunk_heads(tokens):
    return max(1, 256 // tokens)


def stats_kernel(len_ref, cos_ref, sin_ref, q_ref, g_ref, k_ref, v_ref, out_ref):
    count, slots = k_ref.shape[:2]
    tokens = q_ref.shape[0]
    groups = q_ref.shape[1] // HEAD_SIZE
    step = chunk_heads(tokens)
    keys = [rotated(k_ref[p], cos_ref[p], sin_ref[p]) for p in range(count)]
    at = lax.broadcasted_iota(jnp.int32, (slots, step * tokens), 0)
    for h in range(0, groups, step):
        heads = range(h, h + step)
        q2 = head_stack(lambda x: q_ref[:, x * HEAD_SIZE : (x + 1) * HEAD_SIZE], heads)
        g2 = head_stack(lambda x: g_ref[:, x * HEAD_SIZE : (x + 1) * HEAD_SIZE], heads)
        lses, deltas = [], []
        for p in range(count):
            s = mm_nt(keys[p], q2)
            s = jnp.where(at < len_ref[p], s, FILL_VALUE) * (SCALE * LOG2E)
            m = jnp.max(s, axis=0, keepdims=True)
            e = jnp.exp2(s - m)
            total = jnp.sum(e, axis=0, keepdims=True)
            dp = mm_nt(v_ref[p], g2)
            lses.append(m + jnp.log2(total))
            deltas.append(jnp.sum(e * dp, axis=0, keepdims=True) / total)
        lse, delta = merge(jnp.concatenate(lses, axis=0), jnp.concatenate(deltas, axis=0))
        cols = slice(h * tokens, (h + step) * tokens)
        out_ref[0, 0:1, cols] = lse
        out_ref[0, 1:2, cols] = delta


def merge(lses, deltas):
    m = jnp.max(lses, axis=0, keepdims=True)
    w = jnp.exp2(lses - m)
    total = jnp.sum(w, axis=0, keepdims=True)
    return m + jnp.log2(total), jnp.sum(w * deltas, axis=0, keepdims=True) / total


def run_stats(lengths, cos, sin, query, grad, key, val):
    count, slots, feat = key.shape
    kv = feat // HEAD_SIZE
    tokens, width = query.shape
    groups = width // feat
    wide = pl.BlockSpec((tokens, width // kv), lambda g: (0, g))
    thin = pl.BlockSpec((count, slots, HEAD_SIZE), lambda g: (0, 0, g))
    whole = pl.BlockSpec((count, 1, HEAD_SIZE), lambda g: (0, 0, 0))
    return pl.pallas_call(
        stats_kernel,
        grid=(kv,),
        in_specs=[pl.BlockSpec(memory_space=pltpu.SMEM), whole, whole, wide, wide, thin, thin],
        out_specs=pl.BlockSpec((1, 2, groups * tokens), lambda g: (g, 0, 0)),
        out_shape=jax.ShapeDtypeStruct((kv, 2, groups * tokens), F32),
        compiler_params=pltpu.CompilerParams(vmem_limit_bytes=VMEM_LIMIT),
        cost_estimate=pl.CostEstimate(
            flops=4 * count * slots * tokens * width,
            bytes_accessed=4 * count * slots * feat + 4 * tokens * width,
            transcendentals=count * slots * tokens * groups * kv,
        ),
        name="answer_stats",
    )(lengths, cos, sin, query, grad, key, val)


def grads_kernel(
    len_ref, cos_ref, sin_ref, q_ref, g_ref, k_ref, v_ref, stat_ref,
    o_ref, dq_ref, dk_ref, dv_ref, dk_acc, dv_acc,
):
    count, slots = k_ref.shape[:2]
    tokens = q_ref.shape[0]
    groups = q_ref.shape[1] // HEAD_SIZE
    step = chunk_heads(tokens)
    keys = [rotated(k_ref[p], cos_ref[p], sin_ref[p]) for p in range(count)]
    keys_t = [k.T for k in keys]
    vals_t = [v_ref[p].T for p in range(count)]
    at = lax.broadcasted_iota(jnp.int32, (slots, step * tokens), 0)
    for h in range(0, groups, step):
        heads = range(h, h + step)
        cols = slice(h * tokens, (h + step) * tokens)
        q2 = head_stack(lambda x: q_ref[:, x * HEAD_SIZE : (x + 1) * HEAD_SIZE], heads)
        g2 = head_stack(lambda x: g_ref[:, x * HEAD_SIZE : (x + 1) * HEAD_SIZE], heads)
        lse, delta = merge(stat_ref[:, 0, 0, cols], stat_ref[:, 0, 1, cols])
        o_t = dq_t = None
        for p in range(count):
            s = mm_nt(keys[p], q2) * (SCALE * LOG2E)
            prob = jnp.where(at < len_ref[p], jnp.exp2(s - lse), 0.0)
            pb = prob.astype(BF16)
            dp = mm_nt(v_ref[p], g2)
            ds = (prob * (dp - delta)).astype(BF16)
            o_new = mm(vals_t[p], pb)
            dq_new = mm(keys_t[p], ds)
            o_t = o_new if p == 0 else o_t + o_new
            dq_t = dq_new if p == 0 else dq_t + dq_new
            dk_new = mm(ds, q2)
            dv_new = mm(pb, g2)
            if h == 0:
                dk_acc[p] = dk_new
                dv_acc[p] = dv_new
            else:
                dk_acc[p] += dk_new
                dv_acc[p] += dv_new
        o = o_t.T.astype(BF16)
        dq = (dq_t * SCALE).T.astype(BF16)
        for n, x in enumerate(heads):
            out_cols = slice(x * HEAD_SIZE, (x + 1) * HEAD_SIZE)
            o_ref[:, out_cols] = o[n * tokens : (n + 1) * tokens]
            dq_ref[:, out_cols] = dq[n * tokens : (n + 1) * tokens]
    for p in range(count):
        dk = dk_acc[p] * SCALE
        dk = dk * cos_ref[p] - pltpu.roll(dk, HEAD_SIZE // 2, 1) * sin_ref[p]
        dk_ref[p] = dk
        dv_ref[p] = dv_acc[p]


def run_grads(lengths, cos, sin, query, grad, key, val, stats):
    count, slots, feat = key.shape
    kv = feat // HEAD_SIZE
    tokens, width = query.shape
    groups = width // feat
    wide = pl.BlockSpec((tokens, width // kv), lambda g: (0, g))
    thin = pl.BlockSpec((count, slots, HEAD_SIZE), lambda g: (0, 0, g))
    whole = pl.BlockSpec((count, 1, HEAD_SIZE), lambda g: (0, 0, 0))
    stat = pl.BlockSpec((stats.shape[0], 1, 2, groups * tokens), lambda g: (0, g, 0, 0))
    return pl.pallas_call(
        grads_kernel,
        grid=(kv,),
        in_specs=[
            pl.BlockSpec(memory_space=pltpu.SMEM),
            whole, whole, wide, wide, thin, thin, stat,
        ],
        out_specs=[wide, wide, thin, thin],
        out_shape=[
            jax.ShapeDtypeStruct(query.shape, BF16),
            jax.ShapeDtypeStruct(query.shape, BF16),
            jax.ShapeDtypeStruct(key.shape, F32),
            jax.ShapeDtypeStruct(key.shape, F32),
        ],
        scratch_shapes=[pltpu.VMEM((count, slots, HEAD_SIZE), F32)] * 2,
        compiler_params=pltpu.CompilerParams(vmem_limit_bytes=VMEM_LIMIT),
        cost_estimate=pl.CostEstimate(
            flops=12 * count * slots * tokens * width,
            bytes_accessed=16 * count * slots * feat + 8 * tokens * width,
            transcendentals=count * slots * tokens * groups * kv,
        ),
        name="answer_grads",
    )(lengths, cos, sin, query, grad, key, val, stats)


def shards(n_psg, n_row, psg_len, offsets, p_query, passage_key, passage_value, p_grad, a_query, a_grad):
    sent = jnp.concatenate([a_query, a_grad], axis=0)
    sent = jnp.transpose(sent.reshape(sent.shape[0], n_row, -1), (1, 0, 2))
    got = lax.all_to_all(sent, "row", split_axis=0, concat_axis=0, tiled=True)
    got = got.reshape(n_row, 2, n_psg, -1, got.shape[2])
    got = jnp.transpose(got, (1, 2, 0, 3, 4)).reshape(2, -1, got.shape[4])
    queries, grads_in = got[0], got[1]
    tokens, width = queries.shape
    share = tokens // (n_psg * n_row)

    angles = offsets.astype(F32)[:, None, None] * rope_freq(HEAD_SIZE // 2)
    cos = jnp.cos(angles)
    sin = jnp.sin(angles)
    cos = jnp.concatenate([cos, cos], axis=-1)
    sin = jnp.concatenate([-sin, sin], axis=-1)

    stats = run_stats(psg_len, cos, sin, queries, grads_in, passage_key, passage_value)
    stats = lax.all_gather(stats, "psg", axis=0)
    o_part, dq_part, ans_dk, ans_dv = run_grads(
        psg_len, cos, sin, queries, grads_in, passage_key, passage_value, stats
    )
    parts = jnp.concatenate([o_part, dq_part], axis=1)
    parts = lax.all_to_all(parts, ("psg", "row"), split_axis=0, concat_axis=0, tiled=True)

    local_count = p_query.shape[0]
    done = ()
    for index in range(local_count):
        done = run_passage(
            index, psg_len, p_query, passage_key, passage_value, p_grad, ans_dk, ans_dv, done
        )
        if index == 0:
            both = parts.reshape(n_psg, n_row, share, 2, width).astype(F32)
            both = jnp.sum(both, axis=0).astype(BF16)
            both, done = lax.optimization_barrier((both, tuple(done)))
            both = jnp.transpose(both, (2, 1, 0, 3)).reshape(2, share, n_row * width)
            both = lax.all_gather(both, "psg", axis=1, tiled=True)
    p_out, p_dq, p_dk, p_dv = done
    return (p_out, p_dq, p_dk, p_dv, both[0], both[1])


def solution(mesh):
    return jax.shard_map(
        functools.partial(shards, mesh.shape["psg"], mesh.shape["row"]),
        mesh=mesh,
        in_specs=(
            P("psg"),
            P("psg"),
            P("psg", None, "row"),
            P("psg", None, "row"),
            P("psg", None, "row"),
            P("psg", None, "row"),
            P("row", None),
            P("row", None),
        ),
        out_specs=(
            P("psg", None, "row"),
            P("psg", None, "row"),
            P("psg", None, "row"),
            P("psg", None, "row"),
            P("row", None),
            P("row", None),
        ),
        check_vma=False,
    )
```
